1024 devices in a mesh: node: 32 (over z, core), local: 32 (over x, y).
Axes of the slice: x: 4, y: 8, z: 16, core: 2. Of those that a mesh axis runs over, the one named last changes fastest.
Arguments:
- tokens: bfloat16 [131072, 7168], P(('node', 'local')), may hold values from -6 to 6
- route_cot: bfloat16 [12288, 7168], P(('node', 'local')), may hold values from -6 to 6
- expert_ids: int32 [131072, 8], P(('node', 'local')), may hold values from 0 to 255, all different within a row; in each aligned block of 128 rows (0 to 127, 128 to 255, ...) at most 6 rows name the same one
- w_gate: bfloat16 [2, 28672, 512], P(None, 'local'), may hold values from -0.0625 to 0.0625
- w_up: bfloat16 [2, 28672, 512], P(None, 'local'), may hold values from -0.0625 to 0.0625
- w_down: bfloat16 [2, 512, 28672], P(None, None, 'local'), may hold values from -0.125 to 0.125
Outputs:
- route_out: bfloat16 [12288, 7168], P(('node', 'local'))
- route_grad: bfloat16 [12288, 7168], P(('node', 'local'))
The draws below stay inside these ranges and needn't reach their ends.
Inputs may be any that keep to these rules, and one draw needn't show every extreme that they name: `expert_ids`: each row names 8 different experts. Among the 128 tokens of one device no expert is named by more than 6 rows, a bound that some block reaches.
All inputs are finite; a program needn't handle non-finite values.
Results may differ from the reference program's by a relative error of at most 0.006.
Values may be sent and summed in bfloat16 or wider, within the bound.
No kernel may reach another device: no remote copies, remote signals or barrier semaphores. Data moves between devices by JAX's collectives and lax.ppermute only.
A program may use at most 32 MiB of HBM per device.

```python
import math
import jax
import jax.numpy as jnp
import numpy as np
from jax import lax

D = 7168
FF = 2048
EXPERTS = 256
TOP = 8
RESIDENT = 2
TOK_DEV = 128
CAP = 6
DF = 4
TOKENS = 131072
SLOT_ROWS = 12288


def steps_of(key, dims, pieces, low, largest):
    level, own = 1.0, jax.random.fold_in(key, 6)
    for dim, shards_of in pieces:
        draws = jnp.exp(jax.random.uniform(jax.random.fold_in(own, dim), (shards_of,), jnp.float32, low / len(pieces), largest / len(pieces)))
        level = level * jnp.repeat(draws, dims[dim] // shards_of).reshape([-1 if axis == dim else 1 for axis in range(len(dims))])
    return level


def shared_out(rng, own, number, rows, count, top, bound, skew):
    order = jax.random.permutation(rng, count)
    crowded, common = portions_of(count, rows * top, bound, skew, True), portions_of(count, rows * top, bound, skew, False)
    places = jnp.arange(count)

    def named(tallies, offset_by):
        used = int((tallies > 0).sum())
        fixed = max(1, used // 4)
        shifted = fixed + (places - fixed + offset_by * (used - fixed)) % max(1, count - fixed)
        return jnp.zeros((count,), jnp.int32).at[order[jnp.where(places < fixed, places, shifted)]].set(jnp.asarray(tallies, jnp.int32))

    tallies = jnp.where(number % 4 == 0, named(crowded, number // 4), named(common, number - number // 4 - 1))
    mixed = jax.random.permutation(jax.random.fold_in(own, 3), count)
    donor, sink = mixed[0:count // 2 * 2:2], mixed[1:count // 2 * 2:2]
    room = jnp.minimum(tallies[donor] - 1, bound - tallies[sink]) // 2
    room = jnp.where((donor == order[0]) | (sink == order[0]) | (tallies[sink] == 0), 0, jnp.maximum(room, 0))
    shifted = jax.random.randint(jax.random.fold_in(own, 4), (count // 2,), 0, 1 << 20) % (room + 1)
    tallies = tallies.at[donor].add(-shifted).at[sink].add(shifted)
    items = jnp.searchsorted(jnp.cumsum(tallies), jnp.arange(rows * top), side="right").astype(jnp.int32)
    listing = items.reshape(top, rows).T
    listing = listing[jax.random.permutation(jax.random.fold_in(own, 1), rows)]
    offset_by = jax.random.randint(jax.random.fold_in(own, 2), (rows, 1), 0, top)
    return jnp.take_along_axis(listing, (jnp.arange(top)[None, :] + offset_by) % top, axis=1)


def portions_of(amount, total, limit, lean, full):
    loads = [(1 << 20) // math.isqrt(rank ** lean) + 1 for rank in range(1, amount + 1)]
    largest = limit if full else min(limit, max(-(-total // amount), total * loads[0] // sum(loads)))
    least = 1 if total - largest >= amount - 1 else 0
    given, rest = [largest] + [least] * (amount - 1), total - largest - least * (amount - 1)
    while rest > 0:
        candidates = [i for i in range(1, amount) if given[i] < largest] or [i for i in range(1, amount) if given[i] < limit]
        mass, left = sum([loads[i] for i in candidates]), rest
        for i in candidates:
            extra = min(limit - given[i], max(1, left * loads[i] // mass), rest)
            given[i] = given[i] + extra
            rest = rest - extra
    return np.array(given)


def scatter_about(rng, shape, spread, most, split=(), kind=jnp.bfloat16):
    gain = steps_of(rng, shape, split, -0.22, 0.18) if split else 1.0
    drawn = jax.random.normal(rng, shape, jnp.float32) * spread * gain
    return jnp.minimum(jnp.maximum(drawn, -most), most).astype(kind)


def setup_inputs(seed: int = 0) -> dict:
    keys = jax.random.split(jax.random.key(seed), 7)
    tokens = scatter_about(keys[0], (TOKENS, D), 1.0, 6.0, ((0, 1024),))
    route_cot = scatter_about(keys[1], (SLOT_ROWS, D), 1.0, 6.0, ((0, 1024),))
    expert_ids_keys = jax.random.split(jax.random.fold_in(keys[2], 1), TOKENS // TOK_DEV)
    expert_ids_turns = jax.random.permutation(jax.random.fold_in(keys[2], 3), TOKENS // TOK_DEV)
    expert_ids = jax.vmap(lambda own, number: shared_out(jax.random.fold_in(keys[2], 2), own, number, TOK_DEV, EXPERTS, TOP, CAP, 2))(expert_ids_keys, expert_ids_turns).reshape((TOKENS, TOP))
    w_gate = scatter_about(keys[3], (RESIDENT, DF * D, FF // DF), D ** -0.5, 0.0625, ((1, 32),))
    w_up = scatter_about(keys[4], (RESIDENT, DF * D, FF // DF), D ** -0.5, 0.0625, ((1, 32),))
    w_down = scatter_about(keys[5], (RESIDENT, FF // DF, DF * D), FF ** -0.5, 0.125, ((2, 32),))
    return {"tokens": tokens, "route_cot": route_cot, "expert_ids": expert_ids, "w_gate": w_gate, "w_up": w_up, "w_down": w_down}


def silu_parts(values):
    logistic = jax.nn.sigmoid(values)
    return values * logistic, logistic * (1.0 + values * (1.0 - logistic))


def block_total(parts):
    rounded = lax.optimization_barrier(parts.astype(jnp.bfloat16))
    return jnp.sum(rounded.astype(jnp.float32), axis=1).astype(jnp.bfloat16)


def expert_rows(rows_x, rows_cot, first_w, third_w, second_w, first_blocks, third_blocks, second_blocks):
    row_total = rows_x.shape[0]
    block_width = FF // DF
    gate_pre = jnp.dot(rows_x, first_w, preferred_element_type=jnp.float32)
    up_pre = jnp.dot(rows_x, third_w, preferred_element_type=jnp.float32)
    hidden_grad = jnp.dot(rows_cot, second_w.T, preferred_element_type=jnp.float32)
    activation, slope = silu_parts(gate_pre)
    hidden = (activation * up_pre).astype(jnp.bfloat16)
    gate_delta = (hidden_grad * up_pre * slope).astype(jnp.bfloat16)
    up_delta = (hidden_grad * activation).astype(jnp.bfloat16)
    hidden_blocks = hidden.astype(jnp.float32).reshape(row_total, DF, block_width)
    out_parts = jnp.einsum('sbf,bfd->sbd', hidden_blocks, second_blocks)
    gate_blocks = gate_delta.astype(jnp.float32).reshape(row_total, DF, block_width)
    up_blocks = up_delta.astype(jnp.float32).reshape(row_total, DF, block_width)
    back_parts = (jnp.einsum('sbf,dbf->sbd', gate_blocks, first_blocks)
                  + jnp.einsum('sbf,dbf->sbd', up_blocks, third_blocks))
    return block_total(out_parts), block_total(back_parts)


def assemble_in(stored):
    block_width = FF // DF
    return stored.reshape(DF, D, block_width).transpose(1, 0, 2).reshape(D, FF)


def assemble_out(stored):
    block_width = FF // DF
    return stored.reshape(block_width, DF, D).transpose(1, 0, 2).reshape(FF, D)


def first_slots(member_row):
    return jnp.nonzero(member_row, size=CAP, fill_value=0)[0].astype(jnp.int32)


def reference(tokens, route_cot, expert_ids, w_gate, w_up, w_down):
    block_width = FF // DF
    device_total = TOKENS // TOK_DEV
    group_count = min(64, device_total)
    block_tokens = TOK_DEV * group_count
    block_slots = 2 * CAP * group_count
    firsts = [assemble_in(w_gate[q]) for q in range(RESIDENT)]
    thirds = [assemble_in(w_up[q]) for q in range(RESIDENT)]
    seconds = [assemble_out(w_down[q]) for q in range(RESIDENT)]
    first_f = [w.astype(jnp.float32).reshape(D, DF, block_width) for w in firsts]
    third_f = [w.astype(jnp.float32).reshape(D, DF, block_width) for w in thirds]
    second_f = [w.astype(jnp.float32).reshape(DF, block_width, D) for w in seconds]

    def device_block(block_index):
        first_tok = (block_index * block_tokens).astype(jnp.int32)
        first_slot = (block_index * block_slots).astype(jnp.int32)
        block_x = lax.dynamic_slice_in_dim(tokens, first_tok, block_tokens, 0).reshape(group_count, TOK_DEV, D)
        block_ids = lax.dynamic_slice_in_dim(expert_ids, first_tok, block_tokens, 0).reshape(group_count, TOK_DEV, TOP)
        block_cot = lax.dynamic_slice_in_dim(route_cot, first_slot, block_slots, 0).reshape(group_count, 2, CAP, D)
        outs = []
        backs = []
        for q in range(RESIDENT):
            member = jnp.any(block_ids == q, axis=2)
            index = jax.vmap(first_slots)(member)
            count = jnp.sum(member.astype(jnp.int32), axis=1)
            valid = jnp.arange(CAP, dtype=jnp.int32)[None, :] < count[:, None]
            rows_x = jnp.take_along_axis(block_x, index[:, :, None], axis=1).reshape(group_count * CAP, D)
            rows_cot = block_cot[:, q].reshape(group_count * CAP, D)
            expert_out, expert_back = expert_rows(rows_x, rows_cot, firsts[q], thirds[q], seconds[q],
                                                  first_f[q], third_f[q], second_f[q])
            zero = jnp.zeros((), expert_out.dtype)
            outs.append(jnp.where(valid[:, :, None], expert_out.reshape(group_count, CAP, D), zero))
            backs.append(jnp.where(valid[:, :, None], expert_back.reshape(group_count, CAP, D), zero))
        out_block = jnp.stack(outs, axis=1).reshape(block_slots, D)
        back_block = jnp.stack(backs, axis=1).reshape(block_slots, D)
        return out_block, back_block

    starts = jnp.arange(device_total // group_count, dtype=jnp.int32)
    route_out, route_grad = lax.map(device_block, starts)
    return route_out.reshape(SLOT_ROWS, D), route_grad.reshape(SLOT_ROWS, D)
```

```python
import jax
import jax.numpy as jnp
import numpy as np
from jax import lax
from jax.experimental import pallas as pl
from jax.experimental.pallas import tpu as pltpu
from jax.sharding import Mesh, PartitionSpec as P

CAP = 6
XS = 4
YS = 8
SLOTS = 2 * CAP
ROWS = 2 * SLOTS
BF16 = jnp.bfloat16
F32 = jnp.float32


def dot_nn(left, right):
    return jnp.dot(left, right, preferred_element_type=F32)


def dot_nt(left, right):
    return lax.dot_general(
        left, right, (((1,), (1,)), ((), ())), preferred_element_type=F32
    )


def regroup():
    index = np.arange(YS * ROWS).reshape(YS, 2, 2, CAP).transpose(1, 2, 0, 3).reshape(-1)
    return np.eye(YS * ROWS, dtype=np.float32)[index]


def slot_onehot(ids_t, rows):
    count = ids_t.shape[1]
    row = lax.broadcasted_iota(jnp.int32, (rows, count), 0)
    first = row < CAP
    named = [
        jnp.max(jnp.where(ids_t == q, 1.0, 0.0), axis=0, keepdims=True) for q in range(2)
    ]
    member = jnp.where(first, named[0], named[1])
    before = (
        lax.broadcasted_iota(jnp.int32, (count, count), 0)
        < lax.broadcasted_iota(jnp.int32, (count, count), 1)
    )
    position = dot_nn(member.astype(BF16), jnp.where(before, 1.0, 0.0).astype(BF16))
    wanted = jnp.where(first, row, row - CAP).astype(F32)
    hit = (position == wanted) & (member > 0.5) & (row < SLOTS)
    return jnp.where(hit, 1.0, 0.0)


def pack_kernel(ids_ref, tok_ref, cot_ref, out_ref):
    onehot = slot_onehot(ids_ref[...], ROWS).astype(BF16)
    lift = (
        lax.broadcasted_iota(jnp.int32, (ROWS, SLOTS), 0)
        == lax.broadcasted_iota(jnp.int32, (ROWS, SLOTS), 1) + SLOTS
    )
    lift = jnp.where(lift, 1.0, 0.0).astype(BF16)
    width = out_ref.shape[2]
    for s in range(YS):
        cols = slice(s * width, (s + 1) * width)
        out_ref[s] = (
            dot_nn(onehot, tok_ref[:, cols]) + dot_nn(lift, cot_ref[:, cols])
        ).astype(BF16)


def first_kernel(perm_ref, rows_ref, wg_ref, wu_ref, wd_ref, out_ref, lhs_ref):
    block = YS * CAP
    for xs in range(XS):
        moved = dot_nn(perm_ref[...], rows_ref[xs]).astype(BF16)
        for j in range(4):
            lhs_ref[j, pl.ds(xs * block, block), :] = moved[j * block : (j + 1) * block]
    for q in range(2):
        x = lhs_ref[q]
        cot = lhs_ref[2 + q]
        parts = (dot_nn(x, wg_ref[q]), dot_nn(x, wu_ref[q]), dot_nt(cot, wd_ref[q]))
        for j, part in enumerate(parts):
            hidden = part.shape[1]
            out_ref[q * XS : (q + 1) * XS, :, j * hidden : (j + 1) * hidden] = part.astype(
                BF16
            ).reshape(XS, block, hidden)


def act_kernel(sum_ref, out_ref):
    hidden = out_ref.shape[1] // 3

    def total(j):
        cols = slice(j * hidden, (j + 1) * hidden)
        value = sum_ref[0, :, cols].astype(F32)
        for s in range(1, YS):
            value = value + sum_ref[s, :, cols].astype(F32)
        return value

    gate, up, grad = total(0), total(1), total(2)
    logistic = jax.nn.sigmoid(gate)
    activation = gate * logistic
    slope = logistic * (1.0 + gate * (1.0 - logistic))
    out_ref[:, :hidden] = (activation * up).astype(BF16)
    out_ref[:, hidden : 2 * hidden] = (grad * up * slope).astype(BF16)
    out_ref[:, 2 * hidden :] = (grad * activation).astype(BF16)


def second_kernel(back_ref, act_ref, wg_ref, wu_ref, wd_ref, out_ref, res_ref):
    block = YS * CAP
    hidden = act_ref.shape[2] // 3
    for q in range(2):
        mine = act_ref[q * XS : (q + 1) * XS].reshape(XS * block, 3 * hidden)
        out = dot_nn(mine[:, :hidden], wd_ref[q])
        grad = dot_nt(mine[:, hidden : 2 * hidden], wg_ref[q]) + dot_nt(
            mine[:, 2 * hidden :], wu_ref[q]
        )
        for kind, part in enumerate((out, grad)):
            start = (kind * 2 + q) * block
            res_ref[:, pl.ds(start, block), :] = part.astype(BF16).reshape(
                XS, block, part.shape[1]
            )
    for xs in range(XS):
        out_ref[xs] = dot_nn(back_ref[...], res_ref[xs]).astype(BF16)


def sum_kernel(parts_ref, out_ref):
    total = parts_ref[0].astype(F32)
    for i in range(1, XS):
        total = total + parts_ref[i].astype(F32)
    out_ref[...] = total.astype(BF16)


def final_kernel(ids_ref, rows_ref, out_ref, grad_ref):
    valid = jnp.sum(slot_onehot(ids_ref[...], SLOTS), axis=1, keepdims=True) > 0.5
    width = rows_ref.shape[2]
    row = lax.broadcasted_iota(jnp.int32, (SLOTS, ROWS), 0)
    col = lax.broadcasted_iota(jnp.int32, (SLOTS, ROWS), 1)
    pick_out = jnp.where((row == col) & valid, 1.0, 0.0).astype(BF16)
    pick_grad = jnp.where((row + SLOTS == col) & valid, 1.0, 0.0).astype(BF16)
    for s in range(YS):
        cols = slice(s * width, (s + 1) * width)
        out_ref[:, cols] = dot_nn(pick_out, rows_ref[s]).astype(BF16)
        grad_ref[:, cols] = dot_nn(pick_grad, rows_ref[s]).astype(BF16)


def call(kernel, outs, scratch=(), vmem=48):
    spec = pl.BlockSpec(memory_space=pltpu.VMEM)
    single = not isinstance(outs, (tuple, list))

    def run(*args):
        return pl.pallas_call(
            kernel,
            out_shape=outs,
            in_specs=[spec] * len(args),
            out_specs=spec if single else tuple(spec for _ in outs),
            scratch_shapes=list(scratch),
            compiler_params=pltpu.CompilerParams(vmem_limit_bytes=vmem * 1024 * 1024),
        )(*args)

    return run


def on_device(tokens, route_cot, expert_ids, w_gate, w_up, w_down):
    width = tokens.shape[1]
    part = width // YS
    hidden = w_gate.shape[2]
    block = YS * CAP
    ids_t = expert_ids.T
    perm = jnp.asarray(regroup(), BF16)
    back = jnp.asarray(regroup().T, BF16)
    shape = jax.ShapeDtypeStruct

    packed = call(pack_kernel, shape((YS, ROWS, part), BF16))(ids_t, tokens, route_cot)
    sliced = lax.all_to_all(packed, "y", split_axis=0, concat_axis=0, tiled=True)
    rows = lax.all_gather(sliced, "x", axis=0, tiled=False).reshape(XS, YS * ROWS, part)
    partials = call(
        first_kernel,
        shape((2 * XS, block, 3 * hidden), BF16),
        [pltpu.VMEM((4, XS * block, part), BF16)],
    )(perm, rows, w_gate, w_up, w_down)
    shares = lax.all_to_all(partials, "y", split_axis=0, concat_axis=0, tiled=True)
    acts = call(act_kernel, shape((block, 3 * hidden), BF16))(shares)
    gathered = lax.all_gather(acts, "y", axis=0, tiled=False)
    results = call(
        second_kernel,
        shape((XS, YS * ROWS, part), BF16),
        [pltpu.VMEM((XS, YS * ROWS, part), BF16)],
    )(back, gathered, w_gate, w_up, w_down)
    blocks = lax.all_to_all(results, "x", split_axis=0, concat_axis=0, tiled=True)
    total = call(sum_kernel, shape((YS * ROWS, part), BF16))(blocks)
    home = lax.all_to_all(
        total.reshape(YS, ROWS, part), "y", split_axis=0, concat_axis=0, tiled=True
    )
    return call(final_kernel, (shape((SLOTS, width), BF16),) * 2)(ids_t, home)


def solution(mesh):
    nodes = mesh.devices.shape[0]
    grid = Mesh(mesh.devices.reshape(nodes, XS, YS), ("node", "x", "y"))
    rows = P(("node", "x", "y"), None)
    return jax.shard_map(
        on_device,
        mesh=grid,
        in_specs=(
            rows,
            rows,
            rows,
            P(None, ("x", "y"), None),
            P(None, ("x", "y"), None),
            P(None, None, ("x", "y")),
        ),
        out_specs=(rows, rows),
        check_vma=False,
    )
```

```python
import jax
import jax.numpy as jnp
import numpy as np
from jax import lax
from jax.experimental import pallas as pl
from jax.experimental.pallas import tpu as pltpu
from jax.sharding import Mesh, PartitionSpec as P

CAP = 6
XS = 4
YS = 8
SLOTS = 2 * CAP
ROWS = 2 * SLOTS
BF16 = jnp.bfloat16
F32 = jnp.float32


def dot_nn(left, right):
    return jnp.dot(left, right, preferred_element_type=F32)


def dot_nt(left, right):
    return lax.dot_general(
        left, right, (((1,), (1,)), ((), ())), preferred_element_type=F32
    )


def regroup():
    index = np.arange(YS * ROWS).reshape(YS, 2, 2, CAP).transpose(1, 2, 0, 3).reshape(-1)
    return np.eye(YS * ROWS, dtype=np.float32)[index]


def slot_onehot(ids_t, rows):
    count = ids_t.shape[1]
    row = lax.broadcasted_iota(jnp.int32, (rows, count), 0)
    first = row < CAP
    named = [
        jnp.max(jnp.where(ids_t == q, 1.0, 0.0), axis=0, keepdims=True) for q in range(2)
    ]
    member = jnp.where(first, named[0], named[1])
    before = (
        lax.broadcasted_iota(jnp.int32, (count, count), 0)
        < lax.broadcasted_iota(jnp.int32, (count, count), 1)
    )
    position = dot_nn(member.astype(BF16), jnp.where(before, 1.0, 0.0).astype(BF16))
    wanted = jnp.where(first, row, row - CAP).astype(F32)
    hit = (position == wanted) & (member > 0.5) & (row < SLOTS)
    return jnp.where(hit, 1.0, 0.0)


def pack_kernel(ids_any, tok_any, cot_any, out_ref, ids_ref, tok_ref, cot_ref, sems):
    width = out_ref.shape[2]
    small = [
        pltpu.make_async_copy(ids_any, ids_ref, sems.at[YS]),
        pltpu.make_async_copy(cot_any, cot_ref, sems.at[YS + 1]),
    ]
    count = tok_ref.shape[0] // YS
    large = [
        pltpu.make_async_copy(
            tok_any.at[pl.ds(s * count, count)], tok_ref.at[pl.ds(s * count, count)], sems.at[s]
        )
        for s in range(YS)
    ]
    for copy in small + large:
        copy.start()
    for copy in small:
        copy.wait()
    onehot = slot_onehot(ids_ref[...], ROWS).astype(BF16)
    lift = (
        lax.broadcasted_iota(jnp.int32, (ROWS, SLOTS), 0)
        == lax.broadcasted_iota(jnp.int32, (ROWS, SLOTS), 1) + SLOTS
    )
    lift = jnp.where(lift, 1.0, 0.0).astype(BF16)
    for copy in large:
        copy.wait()
    for s in range(YS):
        cols = slice(s * width, (s + 1) * width)
        out_ref[s] = (
            dot_nn(onehot, tok_ref[:, cols]) + dot_nn(lift, cot_ref[:, cols])
        ).astype(BF16)


def copies_kernel(rows_ref, out_ref):
    for xs in range(XS):
        out_ref[xs] = rows_ref[...]


def at(y, step):
    return lax.rem(y + (step + YS), YS)


def first_kernel(
    perm_ref, rows_ref, wg_ref, wu_ref, wd_ref, up_ref, down_ref, keep_ref, lhs_ref, all_ref
):
    block = YS * CAP
    for xs in range(XS):
        moved = dot_nn(perm_ref[...], rows_ref[xs]).astype(BF16)
        for j in range(4):
            lhs_ref[j, pl.ds(xs * block, block), :] = moved[j * block : (j + 1) * block]
    for q in range(2):
        x = lhs_ref[q]
        cot = lhs_ref[2 + q]
        parts = (dot_nn(x, wg_ref[q]), dot_nn(x, wu_ref[q]), dot_nt(cot, wd_ref[q]))
        for j, part in enumerate(parts):
            hidden = part.shape[1]
            all_ref[q * XS : (q + 1) * XS, :, j * hidden : (j + 1) * hidden] = part.reshape(
                XS, block, hidden
            )
    y = lax.axis_index("y")
    half = up_ref.shape[2]
    for ref, sign in ((up_ref, 1), (down_ref, -1)):
        for i, step in enumerate((sign, -2 * sign)):
            for h in range(2):
                ref[2 * i + h] = all_ref[at(y, step), :, h * half : (h + 1) * half].astype(BF16)
    up_ref[4] = all_ref[at(y, 4), :, :half].astype(BF16)
    down_ref[4] = all_ref[at(y, 4), :, half:].astype(BF16)
    for i, step in enumerate((0, 3, -3)):
        keep_ref[i] = all_ref[at(y, step)]


def middle_kernel(keep_ref, below_ref, above_ref, own_ref, up_ref, down_ref):
    half = below_ref.shape[2]
    for h in range(2):
        cols = slice(h * half, (h + 1) * half)
        below = [below_ref[i].astype(F32) for i in (h, 2 + h)]
        above = [above_ref[i].astype(F32) for i in (h, 2 + h)]
        own_ref[:, cols] = keep_ref[0, :, cols] + below[0] + above[0]
        up = keep_ref[1, :, cols] + above[1]
        down = keep_ref[2, :, cols] + below[1]
        if h == 0:
            up = up + below_ref[4].astype(F32)
        else:
            down = down + above_ref[4].astype(F32)
        up_ref[:, cols] = up.astype(BF16)
        down_ref[:, cols] = down.astype(BF16)


def act_kernel(own_ref, below_ref, above_ref, out_ref):
    hidden = out_ref.shape[1] // 3

    def total(j):
        cols = slice(j * hidden, (j + 1) * hidden)
        return (
            own_ref[:, cols] + below_ref[:, cols].astype(F32) + above_ref[:, cols].astype(F32)
        )

    gate, up, grad = total(0), total(1), total(2)
    logistic = jax.nn.sigmoid(gate)
    activation = gate * logistic
    slope = logistic * (1.0 + gate * (1.0 - logistic))
    out_ref[:, :hidden] = (activation * up).astype(BF16)
    out_ref[:, hidden : 2 * hidden] = (grad * up * slope).astype(BF16)
    out_ref[:, 2 * hidden :] = (grad * activation).astype(BF16)


def spread_kernel(own_ref, below_ref, above_ref, up_ref, down_ref):
    half = up_ref.shape[2]
    for h in range(2):
        cols = slice(h * half, (h + 1) * half)
        own, below, above = own_ref[:, cols], below_ref[:, cols], above_ref[:, cols]
        up_ref[h], up_ref[2 + h] = own, above
        down_ref[h], down_ref[2 + h] = own, below
        if h == 0:
            up_ref[4] = below
        else:
            down_ref[4] = above


def second_kernel(
    back_ref,
    own_ref,
    far_below_ref,
    far_above_ref,
    below_ref,
    above_ref,
    wg_ref,
    wu_ref,
    wd_ref,
    out_ref,
    res_ref,
    act_ref,
):
    block = YS * CAP
    hidden = act_ref.shape[2] // 3
    half = below_ref.shape[2]
    y = lax.axis_index("y")
    act_ref[y] = own_ref[...]
    act_ref[at(y, -3)] = far_below_ref[...]
    act_ref[at(y, 3)] = far_above_ref[...]
    for h in range(2):
        cols = slice(h * half, (h + 1) * half)
        act_ref[at(y, -1), :, cols] = below_ref[h]
        act_ref[at(y, 2), :, cols] = below_ref[2 + h]
        act_ref[at(y, 1), :, cols] = above_ref[h]
        act_ref[at(y, -2), :, cols] = above_ref[2 + h]
    act_ref[at(y, 4), :, :half] = below_ref[4]
    act_ref[at(y, 4), :, half:] = above_ref[4]
    for q in range(2):
        mine = act_ref[q * XS : (q + 1) * XS].reshape(XS * block, 3 * hidden)
        out = dot_nn(mine[:, :hidden], wd_ref[q])
        grad = dot_nt(mine[:, hidden : 2 * hidden], wg_ref[q]) + dot_nt(
            mine[:, 2 * hidden :], wu_ref[q]
        )
        for kind, part in enumerate((out, grad)):
            start = (kind * 2 + q) * block
            res_ref[:, pl.ds(start, block), :] = part.astype(BF16).reshape(
                XS, block, part.shape[1]
            )
    for xs in range(XS):
        out_ref[xs] = dot_nn(back_ref[...], res_ref[xs]).astype(BF16)


def sum_kernel(parts_ref, out_ref):
    total = parts_ref[0].astype(F32)
    for i in range(1, XS):
        total = total + parts_ref[i].astype(F32)
    out_ref[...] = total.astype(BF16)


def final_kernel(ids_ref, rows_ref, out_ref, grad_ref):
    valid = jnp.sum(slot_onehot(ids_ref[...], SLOTS), axis=1, keepdims=True) > 0.5
    width = rows_ref.shape[2]
    row = lax.broadcasted_iota(jnp.int32, (SLOTS, ROWS), 0)
    col = lax.broadcasted_iota(jnp.int32, (SLOTS, ROWS), 1)
    pick_out = jnp.where((row == col) & valid, 1.0, 0.0).astype(BF16)
    pick_grad = jnp.where((row + SLOTS == col) & valid, 1.0, 0.0).astype(BF16)
    for s in range(YS):
        cols = slice(s * width, (s + 1) * width)
        out_ref[:, cols] = dot_nn(pick_out, rows_ref[s]).astype(BF16)
        grad_ref[:, cols] = dot_nn(pick_grad, rows_ref[s]).astype(BF16)


def call(kernel, outs, scratch=(), vmem=12, space=pltpu.VMEM):
    spec = pl.BlockSpec(memory_space=pltpu.VMEM)
    single = not isinstance(outs, (tuple, list))

    def run(*args):
        return pl.pallas_call(
            kernel,
            out_shape=outs,
            in_specs=[pl.BlockSpec(memory_space=space)] * len(args),
            out_specs=spec if single else tuple(spec for _ in outs),
            scratch_shapes=list(scratch),
            compiler_params=pltpu.CompilerParams(vmem_limit_bytes=vmem * 1024 * 1024),
        )(*args)

    return run


def shift(value, step):
    return lax.ppermute(value, "y", [(i, (i + step) % YS) for i in range(YS)])


def on_device(tokens, route_cot, expert_ids, w_gate, w_up, w_down):
    width = tokens.shape[1]
    part = width // YS
    hidden = w_gate.shape[2]
    block = YS * CAP
    ids_t = expert_ids.T
    perm = jnp.asarray(regroup(), BF16)
    back = jnp.asarray(regroup().T, BF16)
    shape = jax.ShapeDtypeStruct

    packed = call(
        pack_kernel,
        shape((YS, ROWS, part), BF16),
        [
            pltpu.VMEM(ids_t.shape, jnp.int32),
            pltpu.VMEM(tokens.shape, BF16),
            pltpu.VMEM(route_cot.shape, BF16),
            pltpu.SemaphoreType.DMA((YS + 2,)),
        ],
        vmem=60,
        space=pltpu.HBM,
    )(ids_t, tokens, route_cot)
    sliced = lax.all_to_all(packed, "y", split_axis=0, concat_axis=0, tiled=True)
    rows = lax.all_to_all(
        call(copies_kernel, shape((XS, YS * ROWS, part), BF16))(sliced.reshape(YS * ROWS, part)),
        "x",
        split_axis=0,
        concat_axis=0,
        tiled=True,
    )
    halves = shape((5, block, 3 * hidden // 2), BF16)
    chunk = shape((block, 3 * hidden), BF16)
    up, down, keep = call(
        first_kernel,
        (halves, halves, shape((3, block, 3 * hidden), F32)),
        [
            pltpu.VMEM((4, XS * block, part), BF16),
            pltpu.VMEM((2 * XS, block, 3 * hidden), F32),
        ],
        24,
    )(perm, rows, w_gate, w_up, w_down)
    below, above = shift(up, 1), shift(down, -1)
    own, up, down = call(middle_kernel, (shape(chunk.shape, F32), chunk, chunk))(
        keep, below, above
    )
    below, above = shift(up, 3), shift(down, -3)
    acts = call(act_kernel, chunk)(own, below, above)
    far_below, far_above = shift(acts, 3), shift(acts, -3)
    up, down = call(spread_kernel, (halves, halves))(acts, far_below, far_above)
    below, above = shift(up, 1), shift(down, -1)
    results = call(
        second_kernel,
        shape((XS, YS * ROWS, part), BF16),
        [
            pltpu.VMEM((XS, YS * ROWS, part), BF16),
            pltpu.VMEM((2 * XS, block, 3 * hidden), BF16),
        ],
        24,
    )(back, acts, far_below, far_above, below, above, w_gate, w_up, w_down)
    blocks = lax.all_to_all(results, "x", split_axis=0, concat_axis=0, tiled=True)
    total = call(sum_kernel, shape((YS * ROWS, part), BF16))(blocks)
    home = lax.all_to_all(
        total.reshape(YS, ROWS, part), "y", split_axis=0, concat_axis=0, tiled=True
    )
    return call(final_kernel, (shape((SLOTS, width), BF16),) * 2)(ids_t, home)


def solution(mesh):
    nodes = mesh.devices.shape[0]
    grid = Mesh(mesh.devices.reshape(nodes, XS, YS), ("node", "x", "y"))
    rows = P(("node", "x", "y"), None)
    return jax.shard_map(
        on_device,
        mesh=grid,
        in_specs=(
            rows,
            rows,
            rows,
            P(None, ("x", "y"), None),
            P(None, ("x", "y"), None),
            P(None, None, ("x", "y")),
        ),
        out_specs=(rows, rows),
        check_vma=False,
    )
```

```python
import jax
import jax.numpy as jnp
import numpy as np
from jax import lax
from jax.experimental import pallas as pl
from jax.experimental.pallas import tpu as pltpu
from jax.sharding import Mesh, PartitionSpec as P

CAP = 6
XS = 4
YS = 8
SLOTS = 2 * CAP
ROWS = 2 * SLOTS
BF16 = jnp.bfloat16
F32 = jnp.float32


def dot_nn(left, right):
    return jnp.dot(left, right, preferred_element_type=F32)


def dot_nt(left, right):
    return lax.dot_general(
        left, right, (((1,), (1,)), ((), ())), preferred_element_type=F32
    )


def regroup():
    index = np.arange(YS * ROWS).reshape(YS, 2, 2, CAP).transpose(1, 2, 0, 3).reshape(-1)
    return np.eye(YS * ROWS, dtype=np.float32)[index]


def slot_onehot(ids_t, rows):
    count = ids_t.shape[1]
    row = lax.broadcasted_iota(jnp.int32, (rows, count), 0)
    first = row < CAP
    named = [
        jnp.max(jnp.where(ids_t == q, 1.0, 0.0), axis=0, keepdims=True) for q in range(2)
    ]
    member = jnp.where(first, named[0], named[1])
    before = (
        lax.broadcasted_iota(jnp.int32, (count, count), 0)
        < lax.broadcasted_iota(jnp.int32, (count, count), 1)
    )
    position = dot_nn(member.astype(BF16), jnp.where(before, 1.0, 0.0).astype(BF16))
    wanted = jnp.where(first, row, row - CAP).astype(F32)
    hit = (position == wanted) & (member > 0.5) & (row < SLOTS)
    return jnp.where(hit, 1.0, 0.0)


def pack_kernel(ids_any, tok_any, cot_any, out_ref, ids_ref, tok_ref, cot_ref, sems):
    width = out_ref.shape[2]
    small = [
        pltpu.make_async_copy(ids_any, ids_ref, sems.at[YS]),
        pltpu.make_async_copy(cot_any, cot_ref, sems.at[YS + 1]),
    ]
    count = tok_ref.shape[0] // YS
    large = [
        pltpu.make_async_copy(
            tok_any.at[pl.ds(s * count, count)], tok_ref.at[pl.ds(s * count, count)], sems.at[s]
        )
        for s in range(YS)
    ]
    for copy in small + large:
        copy.start()
    for copy in small:
        copy.wait()
    onehot = slot_onehot(ids_ref[...], ROWS).astype(BF16)
    lift = (
        lax.broadcasted_iota(jnp.int32, (ROWS, SLOTS), 0)
        == lax.broadcasted_iota(jnp.int32, (ROWS, SLOTS), 1) + SLOTS
    )
    lift = jnp.where(lift, 1.0, 0.0).astype(BF16)
    for copy in large:
        copy.wait()
    for s in range(YS):
        cols = slice(s * width, (s + 1) * width)
        out_ref[s] = (
            dot_nn(onehot, tok_ref[:, cols]) + dot_nn(lift, cot_ref[:, cols])
        ).astype(BF16)


def copies_kernel(rows_ref, out_ref):
    for xs in range(XS):
        out_ref[xs] = rows_ref[...]


def first_kernel(perm_ref, rows_ref, wg_ref, wu_ref, wd_ref, out_ref, lhs_ref):
    block = YS * CAP
    for xs in range(XS):
        moved = dot_nn(perm_ref[...], rows_ref[xs]).astype(BF16)
        for j in range(4):
            lhs_ref[j, pl.ds(xs * block, block), :] = moved[j * block : (j + 1) * block]
    for q in range(2):
        x = lhs_ref[q]
        cot = lhs_ref[2 + q]
        parts = (dot_nn(x, wg_ref[q]), dot_nn(x, wu_ref[q]), dot_nt(cot, wd_ref[q]))
        for j, part in enumerate(parts):
            hidden = part.shape[1]
            out_ref[q * XS : (q + 1) * XS, :, j * hidden : (j + 1) * hidden] = part.astype(
                BF16
            ).reshape(XS, block, hidden)


def act_kernel(parts_ref, out_ref):
    hidden = out_ref.shape[2] // 3

    def total(j):
        cols = slice(j * hidden, (j + 1) * hidden)
        value = parts_ref[0, :, cols].astype(F32)
        for s in range(1, YS):
            value = value + parts_ref[s, :, cols].astype(F32)
        return value

    gate, up, grad = total(0), total(1), total(2)
    logistic = jax.nn.sigmoid(gate)
    activation = gate * logistic
    slope = logistic * (1.0 + gate * (1.0 - logistic))
    values = (activation * up, grad * up * slope, grad * activation)
    for j, value in enumerate(values):
        value = value.astype(BF16)
        for s in range(YS):
            out_ref[s, :, j * hidden : (j + 1) * hidden] = value


def second_kernel(back_ref, act_ref, wg_ref, wu_ref, wd_ref, out_ref, res_ref):
    block = YS * CAP
    hidden = act_ref.shape[2] // 3
    for q in range(2):
        mine = act_ref[q * XS : (q + 1) * XS].reshape(XS * block, 3 * hidden)
        out = dot_nn(mine[:, :hidden], wd_ref[q])
        grad = dot_nt(mine[:, hidden : 2 * hidden], wg_ref[q]) + dot_nt(
            mine[:, 2 * hidden :], wu_ref[q]
        )
        for kind, part in enumerate((out, grad)):
            start = (kind * 2 + q) * block
            res_ref[:, pl.ds(start, block), :] = part.astype(BF16).reshape(
                XS, block, part.shape[1]
            )
    for xs in range(XS):
        out_ref[xs] = dot_nn(back_ref[...], res_ref[xs]).astype(BF16)


def sum_kernel(parts_ref, out_ref):
    total = parts_ref[0].astype(F32)
    for i in range(1, XS):
        total = total + parts_ref[i].astype(F32)
    out_ref[...] = total.astype(BF16)


def final_kernel(ids_ref, rows_ref, out_ref, grad_ref):
    valid = jnp.sum(slot_onehot(ids_ref[...], SLOTS), axis=1, keepdims=True) > 0.5
    width = rows_ref.shape[2]
    row = lax.broadcasted_iota(jnp.int32, (SLOTS, ROWS), 0)
    col = lax.broadcasted_iota(jnp.int32, (SLOTS, ROWS), 1)
    pick_out = jnp.where((row == col) & valid, 1.0, 0.0).astype(BF16)
    pick_grad = jnp.where((row + SLOTS == col) & valid, 1.0, 0.0).astype(BF16)
    for s in range(YS):
        cols = slice(s * width, (s + 1) * width)
        out_ref[:, cols] = dot_nn(pick_out, rows_ref[s]).astype(BF16)
        grad_ref[:, cols] = dot_nn(pick_grad, rows_ref[s]).astype(BF16)


def call(kernel, outs, scratch=(), vmem=12, space=pltpu.VMEM):
    spec = pl.BlockSpec(memory_space=pltpu.VMEM)
    single = not isinstance(outs, (tuple, list))

    def run(*args):
        return pl.pallas_call(
            kernel,
            out_shape=outs,
            in_specs=[pl.BlockSpec(memory_space=space)] * len(args),
            out_specs=spec if single else tuple(spec for _ in outs),
            scratch_shapes=list(scratch),
            compiler_params=pltpu.CompilerParams(vmem_limit_bytes=vmem * 1024 * 1024),
        )(*args)

    return run


def send_whole(packed):
    return lax.all_to_all(packed, "y", split_axis=0, concat_axis=0, tiled=True)


def send_in_pieces(packed):
    return jnp.concatenate([send_whole(packed[:, :8]), send_whole(packed[:, 8:])], axis=1)


def on_device(tokens, route_cot, expert_ids, w_gate, w_up, w_down):
    width = tokens.shape[1]
    part = width // YS
    hidden = w_gate.shape[2]
    block = YS * CAP
    ids_t = expert_ids.T
    perm = jnp.asarray(regroup(), BF16)
    back = jnp.asarray(regroup().T, BF16)
    shape = jax.ShapeDtypeStruct

    packed = call(
        pack_kernel,
        shape((YS, ROWS, part), BF16),
        [
            pltpu.VMEM(ids_t.shape, jnp.int32),
            pltpu.VMEM(tokens.shape, BF16),
            pltpu.VMEM(route_cot.shape, BF16),
            pltpu.SemaphoreType.DMA((YS + 2,)),
        ],
        vmem=60,
        space=pltpu.HBM,
    )(ids_t, tokens, route_cot)
    sliced = lax.cond(
        lax.rem(lax.axis_index("node"), 2) == 0, send_in_pieces, send_whole, packed
    )
    rows = lax.all_to_all(
        call(copies_kernel, shape((XS, YS * ROWS, part), BF16))(sliced.reshape(YS * ROWS, part)),
        "x",
        split_axis=0,
        concat_axis=0,
        tiled=True,
    )
    chunks = shape((2 * XS, block, 3 * hidden), BF16)
    partials = call(first_kernel, chunks, [pltpu.VMEM((4, XS * block, part), BF16)], 24)(
        perm, rows, w_gate, w_up, w_down
    )
    shares = lax.all_to_all(partials, "y", split_axis=0, concat_axis=0, tiled=True)
    acts = call(act_kernel, chunks)(shares)
    acts = lax.all_to_all(acts, "y", split_axis=0, concat_axis=0, tiled=True)
    results = call(
        second_kernel,
        shape((XS, YS * ROWS, part), BF16),
        [pltpu.VMEM((XS, YS * ROWS, part), BF16)],
        24,
    )(back, acts, w_gate, w_up, w_down)
    blocks = lax.all_to_all(results, "x", split_axis=0, concat_axis=0, tiled=True)
    total = call(sum_kernel, shape((YS * ROWS, part), BF16))(blocks)
    home = lax.all_to_all(
        total.reshape(YS, ROWS, part), "y", split_axis=0, concat_axis=0, tiled=True
    )
    return call(final_kernel, (shape((SLOTS, width), BF16),) * 2)(ids_t, home)


def solution(mesh):
    nodes = mesh.devices.shape[0]
    grid = Mesh(mesh.devices.reshape(nodes, XS, YS), ("node", "x", "y"))
    rows = P(("node", "x", "y"), None)
    return jax.shard_map(
        on_device,
        mesh=grid,
        in_specs=(
            rows,
            rows,
            rows,
            P(None, ("x", "y"), None),
            P(None, ("x", "y"), None),
            P(None, None, ("x", "y")),
        ),
        out_specs=(rows, rows),
        check_vma=False,
    )
```

```python
import jax
import jax.numpy as jnp
import numpy as np
from jax import lax
from jax.experimental import pallas as pl
from jax.experimental.pallas import tpu as pltpu
from jax.sharding import Mesh, PartitionSpec as P

CAP = 6
XS = 4
YS = 8
SLOTS = 2 * CAP
ROWS = 2 * SLOTS
BF16 = jnp.bfloat16
F32 = jnp.float32


def dot_nn(left, right):
    return jnp.dot(left, right, preferred_element_type=F32)


def dot_nt(left, right):
    return lax.dot_general(
        left, right, (((1,), (1,)), ((), ())), preferred_element_type=F32
    )


def regroup():
    index = np.arange(YS * ROWS).reshape(YS, 2, 2, CAP).transpose(1, 2, 0, 3).reshape(-1)
    return np.eye(YS * ROWS, dtype=np.float32)[index]


def slot_onehot(ids_t, rows):
    count = ids_t.shape[1]
    row = lax.broadcasted_iota(jnp.int32, (rows, count), 0)
    first = row < CAP
    named = [
        jnp.max(jnp.where(ids_t == q, 1.0, 0.0), axis=0, keepdims=True) for q in range(2)
    ]
    member = jnp.where(first, named[0], named[1])
    before = (
        lax.broadcasted_iota(jnp.int32, (count, count), 0)
        < lax.broadcasted_iota(jnp.int32, (count, count), 1)
    )
    position = dot_nn(member.astype(BF16), jnp.where(before, 1.0, 0.0).astype(BF16))
    wanted = jnp.where(first, row, row - CAP).astype(F32)
    hit = (position == wanted) & (member > 0.5) & (row < SLOTS)
    return jnp.where(hit, 1.0, 0.0)


def pack_kernel(ids_any, tok_any, cot_any, out_ref, ids_ref, tok_ref, cot_ref, sems):
    width = out_ref.shape[2]
    small = [
        pltpu.make_async_copy(ids_any, ids_ref, sems.at[YS]),
        pltpu.make_async_copy(cot_any, cot_ref, sems.at[YS + 1]),
    ]
    count = tok_ref.shape[0] // YS
    large = [
        pltpu.make_async_copy(
            tok_any.at[pl.ds(s * count, count)], tok_ref.at[pl.ds(s * count, count)], sems.at[s]
        )
        for s in range(YS)
    ]
    for copy in small + large:
        copy.start()
    for copy in small:
        copy.wait()
    onehot = slot_onehot(ids_ref[...], ROWS).astype(BF16)
    lift = (
        lax.broadcasted_iota(jnp.int32, (ROWS, SLOTS), 0)
        == lax.broadcasted_iota(jnp.int32, (ROWS, SLOTS), 1) + SLOTS
    )
    lift = jnp.where(lift, 1.0, 0.0).astype(BF16)
    for copy in large:
        copy.wait()
    for s in range(YS):
        cols = slice(s * width, (s + 1) * width)
        out_ref[s] = (
            dot_nn(onehot, tok_ref[:, cols]) + dot_nn(lift, cot_ref[:, cols])
        ).astype(BF16)


def copies_kernel(rows_ref, out_ref):
    for xs in range(XS):
        out_ref[xs] = rows_ref[...]


def first_kernel(perm_ref, rows_ref, wg_ref, wu_ref, wd_ref, out_ref, lhs_ref):
    block = YS * CAP
    for xs in range(XS):
        moved = dot_nn(perm_ref[...], rows_ref[xs]).astype(BF16)
        for j in range(4):
            lhs_ref[j, pl.ds(xs * block, block), :] = moved[j * block : (j + 1) * block]
    for q in range(2):
        x = lhs_ref[q]
        cot = lhs_ref[2 + q]
        parts = (dot_nn(x, wg_ref[q]), dot_nn(x, wu_ref[q]), dot_nt(cot, wd_ref[q]))
        for j, part in enumerate(parts):
            hidden = part.shape[1]
            out_ref[q * XS : (q + 1) * XS, :, j * hidden : (j + 1) * hidden] = part.astype(
                BF16
            ).reshape(XS, block, hidden)


def act_kernel(parts_ref, out_ref):
    hidden = out_ref.shape[2] // 3

    def total(j):
        cols = slice(j * hidden, (j + 1) * hidden)
        value = parts_ref[0, :, cols].astype(F32)
        for s in range(1, YS):
            value = value + parts_ref[s, :, cols].astype(F32)
        return value

    gate, up, grad = total(0), total(1), total(2)
    logistic = jax.nn.sigmoid(gate)
    activation = gate * logistic
    slope = logistic * (1.0 + gate * (1.0 - logistic))
    values = (activation * up, grad * up * slope, grad * activation)
    for j, value in enumerate(values):
        value = value.astype(BF16)
        for s in range(YS):
            out_ref[s, :, j * hidden : (j + 1) * hidden] = value


def second_kernel(back_ref, act_ref, wg_ref, wu_ref, wd_ref, out_ref, res_ref):
    block = YS * CAP
    hidden = act_ref.shape[2] // 3
    for q in range(2):
        mine = act_ref[q * XS : (q + 1) * XS].reshape(XS * block, 3 * hidden)
        out = dot_nn(mine[:, :hidden], wd_ref[q])
        grad = dot_nt(mine[:, hidden : 2 * hidden], wg_ref[q]) + dot_nt(
            mine[:, 2 * hidden :], wu_ref[q]
        )
        for kind, part in enumerate((out, grad)):
            start = (kind * 2 + q) * block
            res_ref[:, pl.ds(start, block), :] = part.astype(BF16).reshape(
                XS, block, part.shape[1]
            )
    for xs in range(XS):
        out_ref[xs] = dot_nn(back_ref[...], res_ref[xs]).astype(BF16)


def sum_kernel(parts_ref, out_ref):
    total = parts_ref[0].astype(F32)
    for i in range(1, XS):
        total = total + parts_ref[i].astype(F32)
    out_ref[...] = total.astype(BF16)


def final_kernel(ids_ref, rows_ref, out_ref, grad_ref):
    valid = jnp.sum(slot_onehot(ids_ref[...], SLOTS), axis=1, keepdims=True) > 0.5
    width = rows_ref.shape[2]
    row = lax.broadcasted_iota(jnp.int32, (SLOTS, ROWS), 0)
    col = lax.broadcasted_iota(jnp.int32, (SLOTS, ROWS), 1)
    pick_out = jnp.where((row == col) & valid, 1.0, 0.0).astype(BF16)
    pick_grad = jnp.where((row + SLOTS == col) & valid, 1.0, 0.0).astype(BF16)
    for s in range(YS):
        cols = slice(s * width, (s + 1) * width)
        out_ref[:, cols] = dot_nn(pick_out, rows_ref[s]).astype(BF16)
        grad_ref[:, cols] = dot_nn(pick_grad, rows_ref[s]).astype(BF16)


def call(kernel, outs, scratch=(), vmem=12, space=pltpu.VMEM):
    spec = pl.BlockSpec(memory_space=pltpu.VMEM)
    single = not isinstance(outs, (tuple, list))

    def run(*args):
        return pl.pallas_call(
            kernel,
            out_shape=outs,
            in_specs=[pl.BlockSpec(memory_space=space)] * len(args),
            out_specs=spec if single else tuple(spec for _ in outs),
            scratch_shapes=list(scratch),
            compiler_params=pltpu.CompilerParams(vmem_limit_bytes=vmem * 1024 * 1024),
        )(*args)

    return run


def exchange(value, axis):
    return lax.all_to_all(value, axis, split_axis=0, concat_axis=0, tiled=True)


def copies_of(packed):
    count, width = YS * ROWS, packed.shape[2]
    shape = jax.ShapeDtypeStruct((XS, count, width), BF16)
    return call(copies_kernel, shape)(packed.reshape(count, width))


def dispatch_in_steps(packed):
    return exchange(copies_of(exchange(packed, "y")), "x")


def dispatch_at_once(packed):
    copies = copies_of(packed).reshape(XS * YS, ROWS, packed.shape[2])
    return exchange(copies, ("x", "y")).reshape(XS, YS * ROWS, packed.shape[2])


def products(rows, chunks, perm, w_gate, w_up, w_down):
    block, part = YS * CAP, rows.shape[2]
    return call(first_kernel, chunks, [pltpu.VMEM((4, XS * block, part), BF16)], 24)(
        perm, rows, w_gate, w_up, w_down
    )


def on_device(tokens, route_cot, expert_ids, w_gate, w_up, w_down):
    width = tokens.shape[1]
    part = width // YS
    hidden = w_gate.shape[2]
    block = YS * CAP
    ids_t = expert_ids.T
    perm = jnp.asarray(regroup(), BF16)
    back = jnp.asarray(regroup().T, BF16)
    shape = jax.ShapeDtypeStruct

    packed = call(
        pack_kernel,
        shape((YS, ROWS, part), BF16),
        [
            pltpu.VMEM(ids_t.shape, jnp.int32),
            pltpu.VMEM(tokens.shape, BF16),
            pltpu.VMEM(route_cot.shape, BF16),
            pltpu.SemaphoreType.DMA((YS + 2,)),
        ],
        vmem=60,
        space=pltpu.HBM,
    )(ids_t, tokens, route_cot)
    chunks = shape((2 * XS, block, 3 * hidden), BF16)
    partials = lax.cond(
        lax.rem(lax.axis_index("node"), 2) == 0,
        lambda *args: products(dispatch_in_steps(args[0]), chunks, *args[1:]),
        lambda *args: products(dispatch_at_once(args[0]), chunks, *args[1:]),
        packed,
        perm,
        w_gate,
        w_up,
        w_down,
    )
    shares = lax.all_to_all(partials, "y", split_axis=0, concat_axis=0, tiled=True)
    acts = call(act_kernel, chunks)(shares)
    acts = lax.all_to_all(acts, "y", split_axis=0, concat_axis=0, tiled=True)
    results = call(
        second_kernel,
        shape((XS, YS * ROWS, part), BF16),
        [pltpu.VMEM((XS, YS * ROWS, part), BF16)],
        24,
    )(back, acts, w_gate, w_up, w_down)
    blocks = lax.all_to_all(results, "x", split_axis=0, concat_axis=0, tiled=True)
    total = call(sum_kernel, shape((YS * ROWS, part), BF16))(blocks)
    home = lax.all_to_all(
        total.reshape(YS, ROWS, part), "y", split_axis=0, concat_axis=0, tiled=True
    )
    return call(final_kernel, (shape((SLOTS, width), BF16),) * 2)(ids_t, home)


def solution(mesh):
    nodes = mesh.devices.shape[0]
    grid = Mesh(mesh.devices.reshape(nodes, XS, YS), ("node", "x", "y"))
    rows = P(("node", "x", "y"), None)
    return jax.shard_map(
        on_device,
        mesh=grid,
        in_specs=(
            rows,
            rows,
            rows,
            P(None, ("x", "y"), None),
            P(None, ("x", "y"), None),
            P(None, None, ("x", "y")),
        ),
        out_specs=(rows, rows),
        check_vma=False,
    )
```

```python
import jax
import jax.numpy as jnp
import numpy as np
from jax import lax
from jax.experimental import pallas as pl
from jax.experimental.pallas import tpu as pltpu
from jax.sharding import Mesh, PartitionSpec as P

CAP = 6
XS = 4
YS = 8
SLOTS = 2 * CAP
ROWS = 2 * SLOTS
BF16 = jnp.bfloat16
F32 = jnp.float32


def dot_nn(left, right):
    return jnp.dot(left, right, preferred_element_type=F32)


def dot_nt(left, right):
    return lax.dot_general(
        left, right, (((1,), (1,)), ((), ())), preferred_element_type=F32
    )


def regroup():
    index = np.arange(YS * ROWS).reshape(YS, 2, 2, CAP).transpose(1, 2, 0, 3).reshape(-1)
    return np.eye(YS * ROWS, dtype=np.float32)[index]


def slot_onehot(ids_t, rows):
    count = ids_t.shape[1]
    row = lax.broadcasted_iota(jnp.int32, (rows, count), 0)
    first = row < CAP
    named = [
        jnp.max(jnp.where(ids_t == q, 1.0, 0.0), axis=0, keepdims=True) for q in range(2)
    ]
    member = jnp.where(first, named[0], named[1])
    before = (
        lax.broadcasted_iota(jnp.int32, (count, count), 0)
        < lax.broadcasted_iota(jnp.int32, (count, count), 1)
    )
    position = dot_nn(member.astype(BF16), jnp.where(before, 1.0, 0.0).astype(BF16))
    wanted = jnp.where(first, row, row - CAP).astype(F32)
    hit = (position == wanted) & (member > 0.5) & (row < SLOTS)
    return jnp.where(hit, 1.0, 0.0)


def pack_kernel(ids_any, tok_any, cot_any, out_ref, ids_ref, tok_ref, cot_ref, sems):
    width = out_ref.shape[2]
    small = [
        pltpu.make_async_copy(ids_any, ids_ref, sems.at[YS]),
        pltpu.make_async_copy(cot_any, cot_ref, sems.at[YS + 1]),
    ]
    count = tok_ref.shape[0] // YS
    large = [
        pltpu.make_async_copy(
            tok_any.at[pl.ds(s * count, count)], tok_ref.at[pl.ds(s * count, count)], sems.at[s]
        )
        for s in range(YS)
    ]
    for copy in small + large:
        copy.start()
    for copy in small:
        copy.wait()
    onehot = slot_onehot(ids_ref[...], ROWS).astype(BF16)
    lift = (
        lax.broadcasted_iota(jnp.int32, (ROWS, SLOTS), 0)
        == lax.broadcasted_iota(jnp.int32, (ROWS, SLOTS), 1) + SLOTS
    )
    lift = jnp.where(lift, 1.0, 0.0).astype(BF16)
    for copy in large:
        copy.wait()
    for s in range(YS):
        cols = slice(s * width, (s + 1) * width)
        out_ref[s] = (
            dot_nn(onehot, tok_ref[:, cols]) + dot_nn(lift, cot_ref[:, cols])
        ).astype(BF16)


def copies_kernel(rows_ref, out_ref):
    for xs in range(XS):
        out_ref[xs] = rows_ref[...]


def first_kernel(perm_ref, rows_ref, wg_ref, wu_ref, wd_ref, out_ref, lhs_ref):
    block = YS * CAP
    for xs in range(XS):
        moved = dot_nn(perm_ref[...], rows_ref[xs]).astype(BF16)
        for j in range(4):
            lhs_ref[j, pl.ds(xs * block, block), :] = moved[j * block : (j + 1) * block]
    for q in range(2):
        x = lhs_ref[q]
        cot = lhs_ref[2 + q]
        parts = (dot_nn(x, wg_ref[q]), dot_nn(x, wu_ref[q]), dot_nt(cot, wd_ref[q]))
        for j, part in enumerate(parts):
            hidden = part.shape[1]
            out_ref[q * XS : (q + 1) * XS, :, j * hidden : (j + 1) * hidden] = part.astype(
                BF16
            ).reshape(XS, block, hidden)


def act_kernel(parts_ref, out_ref):
    hidden = out_ref.shape[2] // 3

    def total(j):
        cols = slice(j * hidden, (j + 1) * hidden)
        value = parts_ref[0, :, cols].astype(F32)
        for s in range(1, YS):
            value = value + parts_ref[s, :, cols].astype(F32)
        return value

    gate, up, grad = total(0), total(1), total(2)
    logistic = jax.nn.sigmoid(gate)
    activation = gate * logistic
    slope = logistic * (1.0 + gate * (1.0 - logistic))
    values = (activation * up, grad * up * slope, grad * activation)
    for j, value in enumerate(values):
        value = value.astype(BF16)
        for s in range(YS):
            out_ref[s, :, j * hidden : (j + 1) * hidden] = value


def second_kernel(back_ref, act_ref, wg_ref, wu_ref, wd_ref, out_ref, res_ref):
    block = YS * CAP
    hidden = act_ref.shape[2] // 3
    for q in range(2):
        mine = act_ref[q * XS : (q + 1) * XS].reshape(XS * block, 3 * hidden)
        out = dot_nn(mine[:, :hidden], wd_ref[q])
        grad = dot_nt(mine[:, hidden : 2 * hidden], wg_ref[q]) + dot_nt(
            mine[:, 2 * hidden :], wu_ref[q]
        )
        for kind, part in enumerate((out, grad)):
            start = (kind * 2 + q) * block
            res_ref[:, pl.ds(start, block), :] = part.astype(BF16).reshape(
                XS, block, part.shape[1]
            )
    for xs in range(XS):
        out_ref[xs] = dot_nn(back_ref[...], res_ref[xs]).astype(BF16)


def sum_kernel(parts_ref, out_ref):
    total = parts_ref[0].astype(F32)
    for i in range(1, XS):
        total = total + parts_ref[i].astype(F32)
    out_ref[...] = total.astype(BF16)


def final_kernel(ids_ref, rows_ref, out_ref, grad_ref):
    valid = jnp.sum(slot_onehot(ids_ref[...], SLOTS), axis=1, keepdims=True) > 0.5
    width = rows_ref.shape[2]
    row = lax.broadcasted_iota(jnp.int32, (SLOTS, ROWS), 0)
    col = lax.broadcasted_iota(jnp.int32, (SLOTS, ROWS), 1)
    pick_out = jnp.where((row == col) & valid, 1.0, 0.0).astype(BF16)
    pick_grad = jnp.where((row + SLOTS == col) & valid, 1.0, 0.0).astype(BF16)
    for s in range(YS):
        cols = slice(s * width, (s + 1) * width)
        out_ref[:, cols] = dot_nn(pick_out, rows_ref[s]).astype(BF16)
        grad_ref[:, cols] = dot_nn(pick_grad, rows_ref[s]).astype(BF16)


def call(kernel, outs, scratch=(), vmem=12, space=pltpu.VMEM):
    spec = pl.BlockSpec(memory_space=pltpu.VMEM)
    single = not isinstance(outs, (tuple, list))

    def run(*args):
        return pl.pallas_call(
            kernel,
            out_shape=outs,
            in_specs=[pl.BlockSpec(memory_space=space)] * len(args),
            out_specs=spec if single else tuple(spec for _ in outs),
            scratch_shapes=list(scratch),
            compiler_params=pltpu.CompilerParams(vmem_limit_bytes=vmem * 1024 * 1024),
        )(*args)

    return run


def exchange(value, axis):
    return lax.all_to_all(value, axis, split_axis=0, concat_axis=0, tiled=True)


def copies_of(packed):
    count, width = YS * ROWS, packed.shape[2]
    shape = jax.ShapeDtypeStruct((XS, count, width), BF16)
    return call(copies_kernel, shape)(packed.reshape(count, width))


def dispatch_in_steps(packed):
    return exchange(copies_of(exchange(packed, "y")), "x")


def dispatch_at_once(packed):
    copies = copies_of(packed).reshape(XS * YS, ROWS, packed.shape[2])
    return exchange(copies, ("x", "y")).reshape(XS, YS * ROWS, packed.shape[2])


def products(rows, chunks, perm, w_gate, w_up, w_down):
    block, part = YS * CAP, rows.shape[2]
    return call(first_kernel, chunks, [pltpu.VMEM((4, XS * block, part), BF16)], 24)(
        perm, rows, w_gate, w_up, w_down
    )


def on_device(tokens, route_cot, expert_ids, w_gate, w_up, w_down):
    width = tokens.shape[1]
    part = width // YS
    hidden = w_gate.shape[2]
    block = YS * CAP
    ids_t = expert_ids.T
    perm = jnp.asarray(regroup(), BF16)
    back = jnp.asarray(regroup().T, BF16)
    shape = jax.ShapeDtypeStruct

    packed = call(
        pack_kernel,
        shape((YS, ROWS, part), BF16),
        [
            pltpu.VMEM(ids_t.shape, jnp.int32),
            pltpu.VMEM(tokens.shape, BF16),
            pltpu.VMEM(route_cot.shape, BF16),
            pltpu.SemaphoreType.DMA((YS + 2,)),
        ],
        vmem=60,
        space=pltpu.HBM,
    )(ids_t, tokens, route_cot)
    chunks = shape((2 * XS, block, 3 * hidden), BF16)
    partials = lax.cond(
        lax.rem(lax.axis_index("node"), 2) == 1,
        lambda *args: products(dispatch_in_steps(args[0]), chunks, *args[1:]),
        lambda *args: products(dispatch_at_once(args[0]), chunks, *args[1:]),
        packed,
        perm,
        w_gate,
        w_up,
        w_down,
    )
    shares = lax.all_to_all(partials, "y", split_axis=0, concat_axis=0, tiled=True)
    acts = call(act_kernel, chunks)(shares)
    acts = lax.all_to_all(acts, "y", split_axis=0, concat_axis=0, tiled=True)
    results = call(
        second_kernel,
        shape((XS, YS * ROWS, part), BF16),
        [pltpu.VMEM((XS, YS * ROWS, part), BF16)],
        24,
    )(back, acts, w_gate, w_up, w_down)
    blocks = lax.all_to_all(results, "x", split_axis=0, concat_axis=0, tiled=True)
    total = call(sum_kernel, shape((YS * ROWS, part), BF16))(blocks)
    home = lax.all_to_all(
        total.reshape(YS, ROWS, part), "y", split_axis=0, concat_axis=0, tiled=True
    )
    return call(final_kernel, (shape((SLOTS, width), BF16),) * 2)(ids_t, home)


def solution(mesh):
    nodes = mesh.devices.shape[0]
    grid = Mesh(mesh.devices.reshape(nodes, XS, YS), ("node", "x", "y"))
    rows = P(("node", "x", "y"), None)
    return jax.shard_map(
        on_device,
        mesh=grid,
        in_specs=(
            rows,
            rows,
            rows,
            P(None, ("x", "y"), None),
            P(None, ("x", "y"), None),
            P(None, None, ("x", "y")),
        ),
        out_specs=(rows, rows),
        check_vma=False,
    )
```
